128 devices in a mesh: box: 16 (over x, z), dir: 8 (over y, core).
Axes of the slice: x: 4, y: 4, z: 4, core: 2. Of those that a mesh axis runs over, the one named last changes fastest.
Arguments:
- coeffs: bfloat16 [2, 64, 32, 8, 128], P(None, 'box', 'dir'), may hold values from -6 to 6
- counts: int32 [64, 32], P('box', 'dir'), may hold values from 0 to 128, as said below
- radiation: bfloat16 [2, 64, 32, 128, 128], P(None, 'box', 'dir'), may hold values from -0.5 to 0.5
- near_blocks: bfloat16 [2, 64, 32, 9, 128, 128], P(None, 'box', 'dir'), may hold values from -0.1875 to 0.1875
- trans_leaf: float32 [2, 7, 7, 128], replicated, may hold values from -0.72 to 0.72
- interp: bfloat16 [512, 128], replicated, may hold values from -0.5 to 0.5
- anterp: bfloat16 [128, 512], replicated, may hold values from -0.25 to 0.25
- shift_angle: float32 [4, 512], replicated, may hold values from -3.140625 to 3.140625
- trans_top: float32 [2, 7, 7, 512], P(None, None, None, ('box', 'dir')), may hold values from -0.6 to 0.6
Outputs:
- field: float32 [2, 64, 32, 8, 128], P(None, 'box', 'dir')
The draws below stay inside these ranges and needn't reach their ends.
Inputs may be any that keep to these rules, and one draw needn't show every extreme that they name: `counts`: A box with count 0 is empty; some box holds exactly 128 unknowns.
All inputs are finite; a program needn't handle non-finite values.
Results may differ from the reference program's by a relative error of at most 0.0052.
Values may be sent and summed in bfloat16 or wider, within the bound.
No kernel may reach another device: no remote copies, remote signals or barrier semaphores. Data moves between devices by JAX's collectives and lax.ppermute only.
A program may use at most 128 MiB of HBM per device.

```python
import jax
import jax.numpy as jnp
from jax import lax

PAD = 128
K0 = 128
K1 = 512
RHS = 8
GX = 64
GY = 32
HX = 32
HY = 16


def draw_counts(key, part):
    key = jax.random.fold_in(key, 11)
    first, second, third, fourth = jax.random.split(key, 4)
    base = jax.random.randint(first, (GX, GY), PAD // 4, PAD + 1)
    empty = jax.random.randint(second, (GX, GY), 0, 5) == 0
    full = jax.random.randint(third, (GX, GY), 0, 16) == 0
    result = jnp.where(full, PAD, jnp.where(empty, 0, base)).reshape(-1)
    chosen = jax.random.randint(fourth, (), 0, GX * GY)
    result = result.at[chosen].set(PAD)
    return result.reshape(GX, GY).astype(jnp.int32)


def levels(rng, extent, cuts, smallest, top_value):
    def one(axis_at, blocks):
        steps = jax.random.uniform(jax.random.fold_in(jax.random.fold_in(rng, 6), axis_at), (blocks,), jnp.float32, smallest / len(cuts), top_value / len(cuts))
        return jnp.repeat(jnp.exp(steps), extent[axis_at] // blocks).reshape((-1,) + (1,) * (len(extent) - axis_at - 1))

    loudness = one(*cuts[0])
    for cut in cuts[1:]:
        loudness = loudness * one(*cut)
    return loudness


def scatter_about(rng, dims, width, bound, shards=(), held_as=jnp.bfloat16):
    gain = levels(rng, dims, shards, -0.22, 0.18) if shards else 1.0
    values = jax.random.normal(rng, dims, jnp.float32) * width * gain
    return jnp.minimum(jnp.maximum(values, -bound), bound).astype(held_as)


def setup_inputs(seed: int = 0) -> dict:
    keys = jax.random.split(jax.random.key(seed), 10)
    coeffs = scatter_about(keys[0], (2, GX, GY, RHS, PAD), 1.0, 6.0, ((1, 16), (2, 8)))
    counts = draw_counts(jax.random.fold_in(keys[9], 71), 0)
    radiation = scatter_about(keys[2], (2, GX, GY, PAD, K0), PAD ** -0.5, 0.5, ((1, 16), (2, 8)))
    near_blocks = scatter_about(keys[3], (2, GX, GY, 9, PAD, PAD), (9 * PAD) ** -0.5, 0.1875, ((1, 16), (2, 8)))
    trans_leaf = scatter_about(keys[4], (2, 7, 7, K0), 0.12, 0.72, (), jnp.float32)
    interp = scatter_about(keys[5], (K1, K0), K0 ** -0.5, 0.5)
    anterp = scatter_about(keys[6], (K0, K1), K1 ** -0.5, 0.25)
    shift_angle = jnp.clip(jax.random.uniform(keys[7], (4, K1), jnp.float32, -3.140625, 3.140625), -3.140625, 3.140625)
    trans_top = scatter_about(keys[8], (2, 7, 7, K1), 0.1, 0.6, ((3, 128),), jnp.float32)
    return dict(coeffs=coeffs, counts=counts, radiation=radiation, near_blocks=near_blocks, trans_leaf=trans_leaf, interp=interp, anterp=anterp, shift_angle=shift_angle, trans_top=trans_top)


def far_mask(first, second, shift_x, shift_y):
    par_x = (jnp.arange(first, dtype=jnp.int32) % 2)[:, None]
    par_y = (jnp.arange(second, dtype=jnp.int32) % 2)[None, :]
    keep_x = jnp.abs(jnp.floor_divide(par_x + shift_x, 2)) <= 1
    keep_y = jnp.abs(jnp.floor_divide(par_y + shift_y, 2)) <= 1
    return jnp.where(keep_x & keep_y, 1.0, 0.0).astype(jnp.float32)


def translate(padded, table, first, second):
    total_re = jnp.zeros((first, second) + padded.shape[3:], jnp.float32)
    total_im = jnp.zeros((first, second) + padded.shape[3:], jnp.float32)
    for shift_x in range(-3, 4):
        for shift_y in range(-3, 4):
            if max(abs(shift_x), abs(shift_y)) < 2:
                continue
            source = padded[:, 3 + shift_x:3 + shift_x + first, 3 + shift_y:3 + shift_y + second].astype(jnp.float32)
            weight = far_mask(first, second, shift_x, shift_y)
            weight = weight.reshape(weight.shape + (1,) * (source.ndim - 3))
            coef_re = table[0, shift_x + 3, shift_y + 3]
            coef_im = table[1, shift_x + 3, shift_y + 3]
            total_re = total_re + weight * (coef_re * source[0] - coef_im * source[1])
            total_im = total_im + weight * (coef_re * source[1] + coef_im * source[0])
    return total_re, total_im


def pad_three(values):
    return jnp.pad(values, ((0, 0), (3, 3), (3, 3)) + ((0, 0),) * (values.ndim - 3))


def reference(coeffs, counts, radiation, near_blocks, trans_leaf, interp, anterp, shift_angle, trans_top):
    slots = jnp.arange(PAD, dtype=jnp.int32)
    live = (slots[None, None, None, :] < counts[:, :, None, None]).astype(jnp.float32)
    masked = (coeffs.astype(jnp.float32) * live).astype(jnp.bfloat16)
    padded_near = jnp.pad(masked, ((0, 0), (1, 1), (1, 1), (0, 0), (0, 0)))

    def near_row(row):
        blocks = lax.dynamic_index_in_dim(near_blocks, row, 1, keepdims=False).astype(jnp.float32)
        band = lax.dynamic_slice_in_dim(padded_near, row, 3, 1).astype(jnp.float32)
        shifted = jnp.stack([band[:, sx, sy:sy + GY] for sx in range(3) for sy in range(3)], axis=2)
        out_re = jnp.einsum('jnqp,jnrp->jrq', blocks[0], shifted[0]) - jnp.einsum('jnqp,jnrp->jrq', blocks[1], shifted[1])
        out_im = jnp.einsum('jnqp,jnrp->jrq', blocks[0], shifted[1]) + jnp.einsum('jnqp,jnrp->jrq', blocks[1], shifted[0])
        return jnp.stack([out_re, out_im])

    near = jnp.moveaxis(lax.map(near_row, jnp.arange(GX, dtype=jnp.int32)), 0, 1)

    rad = radiation.astype(jnp.float32)
    values = masked.astype(jnp.float32)
    leaf_re = jnp.einsum('ijpk,ijrp->ijrk', rad[0], values[0]) - jnp.einsum('ijpk,ijrp->ijrk', rad[1], values[1])
    leaf_im = jnp.einsum('ijpk,ijrp->ijrk', rad[0], values[1]) + jnp.einsum('ijpk,ijrp->ijrk', rad[1], values[0])
    leaf = jnp.stack([leaf_re, leaf_im]).astype(jnp.bfloat16)
    far_re, far_im = translate(pad_three(leaf), trans_leaf, GX, GY)

    spread = jnp.einsum('aijrk,ek->aijre', leaf.astype(jnp.float32), interp.astype(jnp.float32))
    cosine = jnp.cos(shift_angle).reshape(2, 1, 2, 1, K1)
    sine = jnp.sin(shift_angle).reshape(2, 1, 2, 1, K1)
    grouped = spread.reshape(2, HX, 2, HY, 2, RHS, K1)
    up_re = jnp.sum(cosine * grouped[0] - sine * grouped[1], axis=(1, 3))
    up_im = jnp.sum(cosine * grouped[1] + sine * grouped[0], axis=(1, 3))
    upper = jnp.stack([up_re, up_im]).astype(jnp.bfloat16)

    top_re, top_im = translate(pad_three(upper), trans_top, HX, HY)
    top = jnp.stack([top_re, top_im]).astype(jnp.bfloat16)
    parent = top.astype(jnp.float32)[:, :, None, :, None]
    down_re = (cosine * parent[0] + sine * parent[1]).reshape(GX, GY, RHS, K1)
    down_im = (cosine * parent[1] - sine * parent[0]).reshape(GX, GY, RHS, K1)
    down = jnp.stack([down_re, down_im]).astype(jnp.bfloat16)
    back = jnp.einsum('aijre,ke->aijrk', down.astype(jnp.float32), anterp.astype(jnp.float32))
    total = (jnp.stack([far_re, far_im]) + back).astype(jnp.bfloat16)

    incoming = total.astype(jnp.float32)
    recv_re = jnp.einsum('ijpk,ijrk->ijrp', rad[0], incoming[0]) + jnp.einsum('ijpk,ijrk->ijrp', rad[1], incoming[1])
    recv_im = jnp.einsum('ijpk,ijrk->ijrp', rad[0], incoming[1]) - jnp.einsum('ijpk,ijrk->ijrp', rad[1], incoming[0])
    return jnp.stack([near[0] + recv_re, near[1] + recv_im]) * live[None]
```

```python
import jax
import jax.numpy as jnp
from jax import lax
from jax.experimental import pallas as pl
from jax.experimental.pallas import tpu as pltpu
from jax.sharding import PartitionSpec as P

OWN, EDGE, SIDE = 48, 28, 70
NT = (((1,), (1,)), ((), ()))
F32 = jnp.float32
BF16 = jnp.bfloat16
LINK = F32
LEAF_VMEM = 62 << 20


def dot_nt(left, right):
    return lax.dot_general(left, right, NT, preferred_element_type=F32)


def pair(real, imag):
    return jnp.concatenate([real, imag], axis=0)


def vmem():
    return pl.BlockSpec(memory_space=pltpu.VMEM)


def smem():
    return pl.BlockSpec(memory_space=pltpu.SMEM)


def hbm():
    return pl.BlockSpec(memory_space=pl.ANY)


def params(mib):
    return pltpu.CompilerParams(vmem_limit_bytes=mib << 20)


def cost(us):
    return pl.CostEstimate(flops=us * 10**9, bytes_accessed=us << 20, transcendentals=0)


def leaf_kernel(
    counts_hbm,
    coeffs_hbm,
    radiation,
    interp_hbm,
    angle_hbm,
    table_hbm,
    own,
    up,
    down,
    phase,
    piece,
    counts,
    coeffs,
    rad,
    interp,
    angle,
    table,
    sems,
    rad_sems,
):
    small = [
        pltpu.make_async_copy(counts_hbm, counts, sems.at[0]),
        pltpu.make_async_copy(coeffs_hbm, coeffs, sems.at[1]),
        pltpu.make_async_copy(angle_hbm, angle, sems.at[2]),
        pltpu.make_async_copy(interp_hbm, interp, sems.at[3]),
        pltpu.make_async_copy(table_hbm, table, sems.at[4]),
    ]
    copies = [
        pltpu.make_async_copy(radiation.at[:, i], rad.at[:, i], rad_sems.at[i]) for i in range(4)
    ]
    for copy in small + copies:
        copy.start()
    for copy in small:
        copy.wait()
    cosine = jnp.cos(angle[...])
    sine = jnp.sin(angle[...])
    phase[0:4, :] = cosine
    phase[4:8, :] = sine
    piece[...] = jnp.zeros_like(piece)
    for part in range(2):
        for dx in range(7):
            at = (part * 7 + dx) * 8
            piece[:, at : at + 7] = table[part, dx].astype(piece.dtype)
    lane = lax.broadcasted_iota(jnp.int32, (16, 128), 1)
    leaves = []
    for copy in copies:
        copy.wait()
    for i in range(4):
        for j in range(4):
            both = pair(coeffs[0, i, j].astype(F32), coeffs[1, i, j].astype(F32))
            masked = jnp.where(lane < counts[i, j], both, 0.0).astype(BF16)
            wide = jnp.concatenate([rad[0, i, j], rad[1, i, j]], axis=1)
            prod = jnp.dot(masked, wide, preferred_element_type=F32)
            first, second = prod[:, 0:128], prod[:, 128:256]
            leaf = pair(first[0:8] - second[8:16], first[8:16] + second[0:8]).astype(BF16)
            leaves.append(leaf)
            own[j * 4 + i] = leaf
            own[16 + j * 4 + i] = masked
            if i < 2:
                down[j * 2 + i] = leaf
            else:
                up[j * 2 + i - 2] = leaf
            if i == 0:
                down[8 + j] = masked
            if i == 3:
                up[8 + j] = masked
    spread = dot_nt(jnp.concatenate(leaves, axis=0), interp[...])
    for big_i in range(2):
        for big_j in range(2):
            real = imag = None
            for a in range(2):
                for b in range(2):
                    at = ((2 * big_i + a) * 4 + 2 * big_j + b) * 16
                    s_re, s_im = spread[at : at + 8], spread[at + 8 : at + 16]
                    c = cosine[2 * a + b : 2 * a + b + 1]
                    s = sine[2 * a + b : 2 * a + b + 1]
                    t_re = c * s_re - s * s_im
                    t_im = c * s_im + s * s_re
                    real = t_re if real is None else real + t_re
                    imag = t_im if imag is None else imag + t_im
            upper = pair(real, imag).astype(BF16)
            for t in range(4):
                unit = (big_i * 2 + big_j) * 4 + t
                tile = upper[:, t * 128 : (t + 1) * 128]
                own[32 + unit] = tile
                up[12 + unit] = tile
                down[12 + unit] = tile


def pieces_kernel(piece, pieces):
    pieces[...] = jnp.broadcast_to(piece[...][None], pieces.shape)


def pack_kernel(own, before, after, right, left, sem):
    copies = []
    for target, col in ((right, 2), (left, 0)):
        edge_col = 3 if col else 0
        moves = [
            (before.at[pl.ds(col * 2, 4)], 0, 4),
            (own.at[pl.ds(col * 4, 8)], 4, 8),
            (after.at[pl.ds(col * 2, 4)], 12, 4),
            (before.at[pl.ds(8 + edge_col, 1)], 16, 1),
            (own.at[pl.ds(16 + edge_col * 4, 4)], 17, 4),
            (after.at[pl.ds(8 + edge_col, 1)], 21, 1),
            (before.at[pl.ds(12, 16)], 22, 16),
            (own.at[pl.ds(32, 16)], 38, 16),
            (after.at[pl.ds(12, 16)], 54, 16),
        ]
        for source, at, size in moves:
            copies.append((source, target.at[pl.ds(at, size)]))
    started = [
        pltpu.make_async_copy(source, target, sem.at[index])
        for index, (source, target) in enumerate(copies)
    ]
    for copy in started:
        copy.start()
    for copy in started:
        copy.wait()


def near_sum(masks, real_blocks, imag_blocks):
    row = jnp.concatenate(masks, axis=1)
    first = dot_nt(row, jnp.concatenate(real_blocks, axis=1))
    second = dot_nt(row, jnp.concatenate(imag_blocks, axis=1))
    return pair(first[0:8] - second[8:16], first[8:16] + second[0:8])


def inside(j):
    return [dy for dy in (-1, 0, 1) if 0 <= j + dy < 4]


def near_kernel(own, before, after, blocks, out, held, sems):
    copies = []
    for i in range(4):
        group = [pltpu.make_async_copy(blocks.at[:, i, 1:3], held.at[:, i, 1:3], sems.at[i, 0])]
        for j, low in ((0, 1), (3, 0)):
            for dx in range(3):
                span = pl.ds(3 * dx + low, 2)
                group.append(
                    pltpu.make_async_copy(
                        blocks.at[:, i, j, span], held.at[:, i, j, span], sems.at[i, len(group)]
                    )
                )
        copies.append(group)
    for group in copies:
        for copy in group:
            copy.start()
    here = lax.axis_index("box")
    has_before = (here > 0).astype(F32)
    has_after = (here < lax.axis_size("box") - 1).astype(F32)
    rows = {}
    for j in range(4):
        rows[-1, j] = (before[8 + j].astype(F32) * has_before).astype(BF16)
        rows[4, j] = (after[8 + j].astype(F32) * has_after).astype(BF16)
        for i in range(4):
            rows[i, j] = own[16 + j * 4 + i]
    for i in range(4):
        for copy in copies[i]:
            copy.wait()
        for j in range(4):
            pairs = [(dx, dy) for dx in (-1, 0, 1) for dy in inside(j)]
            out[i * 4 + j] = near_sum(
                [rows[i + dx, j + dy] for dx, dy in pairs],
                [held[0, i, j, 3 * (dx + 1) + dy + 1] for dx, dy in pairs],
                [held[1, i, j, 3 * (dx + 1) + dy + 1] for dx, dy in pairs],
            )


def translate(source, coef, keep):
    total = {}
    for r in range(6):
        for c in range(6):
            unit = source(r, c)
            s_re, s_im = unit[0:8], unit[8:16]
            for a in range(2):
                for b in range(2):
                    dx, dy = r - 2 - a, c - 2 - b
                    if max(abs(dx), abs(dy)) < 2:
                        continue
                    k_re, k_im = coef(0, dx, dy), coef(1, dx, dy)
                    t_re = k_re * s_re - k_im * s_im
                    t_im = k_re * s_im + k_im * s_re
                    if (a, b) in total:
                        old_re, old_im = total[a, b]
                        t_re, t_im = old_re + t_re, old_im + t_im
                    total[a, b] = (t_re, t_im)
    for (a, b), (t_re, t_im) in total.items():
        keep(a, b, pair(t_re, t_im))


def final_kernel(
    counts,
    own,
    before,
    after,
    left,
    right,
    pieces,
    trans_leaf,
    anterp,
    phase,
    near,
    rad,
    blocks,
    out,
    rest,
    leaf_halo,
    upper_halo,
    table,
    far,
    top,
    sems,
):
    copies = []
    for i in range(4):
        for dx in range(3):
            for side, (j, n) in enumerate(((0, 3 * dx), (3, 3 * dx + 2))):
                slot = (i * 3 + dx) * 2 + side
                copies.append(
                    pltpu.make_async_copy(blocks.at[:, i, j, n], rest.at[:, slot], sems.at[slot])
                )
    for copy in copies:
        copy.start()
    box, col = lax.axis_index("box"), lax.axis_index("dir")
    f_before = (box > 0).astype(F32)
    f_after = (box < lax.axis_size("box") - 1).astype(F32)
    f_left = (col > 0).astype(F32)
    f_right = (col < lax.axis_size("dir") - 1).astype(F32)

    for j in range(4):
        for r in range(2):
            leaf_halo[r * 8 + j + 2] = before[j * 2 + r].astype(F32) * f_before
            leaf_halo[(r + 6) * 8 + j + 2] = after[j * 2 + r].astype(F32) * f_after
        for i in range(4):
            leaf_halo[(i + 2) * 8 + j + 2] = own[j * 4 + i].astype(F32)
    for part, flag, start in ((left, f_left, 0), (right, f_right, 6)):
        for c in range(2):
            for r in range(2):
                leaf_halo[r * 8 + start + c] = part[c * 2 + r].astype(F32) * (flag * f_before)
                leaf_halo[(r + 6) * 8 + start + c] = part[12 + c * 2 + r].astype(F32) * (
                    flag * f_after
                )
            for i in range(4):
                leaf_halo[(i + 2) * 8 + start + c] = part[4 + c * 4 + i].astype(F32) * flag
    for p in range(2):
        for q in range(2):
            for t in range(4):
                unit = (p * 2 + q) * 4 + t
                upper_halo[t, p * 6 + q + 2] = before[12 + unit].astype(F32) * f_before
                upper_halo[t, (p + 2) * 6 + q + 2] = own[32 + unit].astype(F32)
                upper_halo[t, (p + 4) * 6 + q + 2] = after[12 + unit].astype(F32) * f_after
                for part, flag, start in ((left, f_left, 0), (right, f_right, 4)):
                    upper_halo[t, p * 6 + q + start] = part[22 + unit].astype(F32) * (
                        flag * f_before
                    )
                    upper_halo[t, (p + 2) * 6 + q + start] = part[38 + unit].astype(F32) * flag
                    upper_halo[t, (p + 4) * 6 + q + start] = part[54 + unit].astype(F32) * (
                        flag * f_after
                    )
    for t in range(4):
        table[t] = pieces[pl.ds(t * 32, 32)].astype(F32).reshape(128, 128).T

    def leaf_step(quad, carry):
        base = (quad // 2) * 16 + (quad % 2) * 2

        def keep(a, b, value):
            far[quad * 4 + a * 2 + b] = value

        translate(
            lambda r, c: leaf_halo[base + r * 8 + c],
            lambda part, dx, dy: trans_leaf[dx + 3, dy + 3, pl.ds(part, 1), :],
            keep,
        )
        return carry

    def top_step(t, carry):
        def keep(a, b, value):
            top[t, a * 2 + b] = value.astype(BF16).astype(F32)

        translate(
            lambda r, c: upper_halo[t, r * 6 + c],
            lambda part, dx, dy: table[t, pl.ds((part * 7 + dx + 3) * 8 + dy + 3, 1), :],
            keep,
        )
        return carry

    lax.fori_loop(0, 4, leaf_step, 0)
    lax.fori_loop(0, 4, top_step, 0)

    rows = []
    for quad in range(4):
        for child in range(4):
            tiles = []
            for t in range(4):
                unit = top[t, quad]
                t_re, t_im = unit[0:8], unit[8:16]
                c = phase[child : child + 1, t * 128 : (t + 1) * 128]
                s = phase[4 + child : 5 + child, t * 128 : (t + 1) * 128]
                tiles.append(pair(c * t_re + s * t_im, c * t_im - s * t_re).astype(BF16))
            rows.append(jnp.concatenate(tiles, axis=1))
    back = dot_nt(jnp.concatenate(rows, axis=0), anterp[...])
    lane = lax.broadcasted_iota(jnp.int32, (16, 128), 1)
    for copy in copies:
        copy.wait()

    def side_mask(part, flag, i):
        if i < 0:
            return (part[16].astype(F32) * (flag * f_before)).astype(BF16)
        if i > 3:
            return (part[21].astype(F32) * (flag * f_after)).astype(BF16)
        return (part[17 + i].astype(F32) * flag).astype(BF16)

    sides = {}
    for i in range(-1, 5):
        sides[0, i] = side_mask(left, f_left, i)
        sides[3, i] = side_mask(right, f_right, i)
    for i in range(4):
        for j in range(4):
            at = ((i // 2) * 2 + j // 2) * 4 + (i % 2) * 2 + j % 2
            total = (far[at] + back[at * 16 : at * 16 + 16]).astype(BF16)
            both = dot_nt(total, rad[:, i, j].reshape(256, 128))
            first, second = both[:, 0:128], both[:, 128:256]
            field = near[i * 4 + j] + pair(
                first[0:8] + second[8:16], first[8:16] - second[0:8]
            )
            if j in (0, 3):
                slots = [(i * 3 + dx) * 2 + (1 if j else 0) for dx in range(3)]
                field = field + near_sum(
                    [sides[j, i + dx] for dx in (-1, 0, 1)],
                    [rest[0, slot] for slot in slots],
                    [rest[1, slot] for slot in slots],
                )
            field = jnp.where(lane < counts[i, j], field, 0.0)
            out[0, i, j] = field[0:8]
            out[1, i, j] = field[8:16]


def unit_shape(count):
    return jax.ShapeDtypeStruct((count, 16, 128), BF16)


def shards(
    coeffs, counts, radiation, near_blocks, trans_leaf, interp, anterp, shift_angle, trans_top
):
    n_box = lax.axis_size("box")
    n_dir = lax.axis_size("dir")
    devices = n_box * n_dir
    own, to_after, to_before, phase, piece = pl.pallas_call(
        leaf_kernel,
        out_shape=(
            unit_shape(OWN),
            unit_shape(EDGE),
            unit_shape(EDGE),
            jax.ShapeDtypeStruct((8, 512), F32),
            jax.ShapeDtypeStruct((4, 128), LINK),
        ),
        in_specs=[hbm()] * 6,
        out_specs=(vmem(),) * 5,
        scratch_shapes=[
            pltpu.SMEM((4, 4), jnp.int32),
            pltpu.VMEM((2, 4, 4, 8, 128), BF16),
            pltpu.VMEM((2, 4, 4, 128, 128), BF16),
            pltpu.VMEM((512, 128), BF16),
            pltpu.VMEM((4, 512), F32),
            pltpu.VMEM((2, 7, 4, 7), F32),
            pltpu.SemaphoreType.DMA((5,)),
            pltpu.SemaphoreType.DMA((4,)),
        ],
        compiler_params=pltpu.CompilerParams(vmem_limit_bytes=LEAF_VMEM),
        cost_estimate=cost(2),
        name="leaf",
    )(counts, coeffs, radiation, interp, shift_angle, trans_top.transpose(0, 1, 3, 2))
    forward = [(i, (i + 1) % n_box) for i in range(n_box)]
    backward = [((i + 1) % n_box, i) for i in range(n_box)]
    before = lax.ppermute(to_after, "box", forward)
    after = lax.ppermute(to_before, "box", backward)
    pieces = pl.pallas_call(
        pieces_kernel,
        out_shape=jax.ShapeDtypeStruct((devices, 4, 128), LINK),
        in_specs=[vmem()],
        out_specs=vmem(),
        compiler_params=params(4),
        cost_estimate=cost(20),
        name="pieces",
    )(piece)
    gathered = lax.all_to_all(pieces, ("box", "dir"), split_axis=0, concat_axis=0, tiled=True)
    to_right, to_left = pl.pallas_call(
        pack_kernel,
        out_shape=(unit_shape(SIDE), unit_shape(SIDE)),
        in_specs=[hbm()] * 3,
        out_specs=(hbm(),) * 2,
        scratch_shapes=[pltpu.SemaphoreType.DMA((18,))],
        compiler_params=params(4),
        cost_estimate=cost(20),
        name="pack",
    )(own, before, after)
    left = lax.ppermute(to_right, "dir", [(i, (i + 1) % n_dir) for i in range(n_dir)])
    right = lax.ppermute(to_left, "dir", [((i + 1) % n_dir, i) for i in range(n_dir)])
    near = pl.pallas_call(
        near_kernel,
        out_shape=jax.ShapeDtypeStruct((16, 16, 128), F32),
        in_specs=[vmem()] * 3 + [hbm()],
        out_specs=vmem(),
        scratch_shapes=[
            pltpu.VMEM((2, 4, 4, 9, 128, 128), BF16),
            pltpu.SemaphoreType.DMA((4, 7)),
        ],
        compiler_params=params(48),
        cost_estimate=cost(4),
        name="near",
    )(own, before, after, near_blocks)
    return pl.pallas_call(
        final_kernel,
        out_shape=jax.ShapeDtypeStruct((2, 4, 4, 8, 128), F32),
        in_specs=[smem()] + [vmem()] * 11 + [hbm()],
        out_specs=vmem(),
        scratch_shapes=[
            pltpu.VMEM((2, 24, 128, 128), BF16),
            pltpu.VMEM((64, 16, 128), F32),
            pltpu.VMEM((4, 36, 16, 128), F32),
            pltpu.VMEM((4, 128, 128), F32),
            pltpu.VMEM((16, 16, 128), F32),
            pltpu.VMEM((4, 4, 16, 128), F32),
            pltpu.SemaphoreType.DMA((24,)),
        ],
        compiler_params=params(48),
        cost_estimate=cost(4),
        name="final",
    )(
        counts,
        own,
        before,
        after,
        left,
        right,
        gathered,
        trans_leaf.transpose(1, 2, 0, 3),
        anterp,
        phase,
        near,
        radiation,
        near_blocks,
    )


def solution(mesh):
    return jax.shard_map(
        shards,
        mesh=mesh,
        in_specs=(
            P(None, "box", "dir", None, None),
            P("box", "dir"),
            P(None, "box", "dir", None, None),
            P(None, "box", "dir", None, None, None),
            P(),
            P(),
            P(),
            P(),
            P(None, None, None, ("box", "dir")),
        ),
        out_specs=P(None, "box", "dir", None, None),
        check_vma=False,
    )
```

```python
import jax
import jax.numpy as jnp
from jax import lax
from jax.experimental import pallas as pl
from jax.experimental.pallas import tpu as pltpu
from jax.sharding import PartitionSpec as P

OWN, EDGE, SIDE = 48, 28, 70
NT = (((1,), (1,)), ((), ()))
F32 = jnp.float32
BF16 = jnp.bfloat16


def dot_nt(left, right):
    return lax.dot_general(left, right, NT, preferred_element_type=F32)


def pair(real, imag):
    return jnp.concatenate([real, imag], axis=0)


def vmem():
    return pl.BlockSpec(memory_space=pltpu.VMEM)


def hbm():
    return pl.BlockSpec(memory_space=pl.ANY)


def params(mib):
    return pltpu.CompilerParams(vmem_limit_bytes=mib << 20)


def cost(us):
    return pl.CostEstimate(flops=us * 10**9, bytes_accessed=us << 20, transcendentals=0)


def leaf_kernel(
    counts_hbm,
    coeffs_hbm,
    radiation,
    interp_hbm,
    angle_hbm,
    table_hbm,
    own_hbm,
    up_hbm,
    down_hbm,
    phase_hbm,
    live_hbm,
    pieces_hbm,
    counts,
    coeffs,
    rad,
    interp,
    angle,
    table,
    own,
    up,
    down,
    phase,
    live,
    pieces,
    sems,
    rad_sems,
    out_sems,
):
    counts_in = pltpu.make_async_copy(counts_hbm, counts, sems.at[0])
    coeffs_in = pltpu.make_async_copy(coeffs_hbm, coeffs, sems.at[1])
    angle_in = pltpu.make_async_copy(angle_hbm, angle, sems.at[2])
    table_in = pltpu.make_async_copy(table_hbm, table, sems.at[3])
    interp_in = pltpu.make_async_copy(interp_hbm, interp, sems.at[4])
    rad_in = [
        pltpu.make_async_copy(radiation.at[:, i], rad.at[:, i], rad_sems.at[i]) for i in range(4)
    ]
    for copy in (table_in, angle_in, counts_in, coeffs_in, *rad_in, interp_in):
        copy.start()
    sent = []

    def send(source, target):
        copy = pltpu.make_async_copy(source, target, out_sems.at[len(sent)])
        copy.start()
        sent.append(copy)

    pieces[0] = jnp.zeros((4, 128), F32)
    table_in.wait()
    for part in range(2):
        for dx in range(7):
            at = (part * 7 + dx) * 8
            pieces[0, :, at : at + 7] = table[part, dx]
    pieces[...] = jnp.broadcast_to(pieces[0:1], pieces.shape)
    send(pieces, pieces_hbm)
    angle_in.wait()
    cosine = jnp.cos(angle[...])
    sine = jnp.sin(angle[...])
    phase[0:4, :] = cosine
    phase[4:8, :] = sine
    send(phase, phase_hbm)
    counts_in.wait()
    lane = lax.broadcasted_iota(jnp.int32, (8, 128), 1)
    for i in range(4):
        for j in range(4):
            live[i * 4 + j] = (lane < counts[i, j]).astype(F32)
    send(live, live_hbm)
    coeffs_in.wait()
    for copy in rad_in:
        copy.wait()
    leaves = []
    for i in range(4):
        for j in range(4):
            on = live[i * 4 + j]
            masked = pair(
                coeffs[0, i, j].astype(F32) * on, coeffs[1, i, j].astype(F32) * on
            ).astype(BF16)
            wide = jnp.concatenate([rad[0, i, j], rad[1, i, j]], axis=1)
            prod = jnp.dot(masked, wide, preferred_element_type=F32)
            first, second = prod[:, 0:128], prod[:, 128:256]
            leaf = pair(first[0:8] - second[8:16], first[8:16] + second[0:8]).astype(BF16)
            leaves.append(leaf)
            own[j * 4 + i] = leaf
            own[16 + j * 4 + i] = masked
            if i < 2:
                down[j * 2 + i] = leaf
            else:
                up[j * 2 + i - 2] = leaf
            if i == 0:
                down[8 + j] = masked
            if i == 3:
                up[8 + j] = masked
    for source, target, count in ((up, up_hbm, 12), (down, down_hbm, 12), (own, own_hbm, 32)):
        send(source.at[pl.ds(0, count)], target.at[pl.ds(0, count)])
    interp_in.wait()
    spread = dot_nt(jnp.concatenate(leaves, axis=0), interp[...])
    for big_i in range(2):
        for big_j in range(2):
            real = imag = None
            for a in range(2):
                for b in range(2):
                    at = ((2 * big_i + a) * 4 + 2 * big_j + b) * 16
                    s_re, s_im = spread[at : at + 8], spread[at + 8 : at + 16]
                    c = cosine[2 * a + b : 2 * a + b + 1]
                    s = sine[2 * a + b : 2 * a + b + 1]
                    t_re = c * s_re - s * s_im
                    t_im = c * s_im + s * s_re
                    real = t_re if real is None else real + t_re
                    imag = t_im if imag is None else imag + t_im
            upper = pair(real, imag).astype(BF16)
            for t in range(4):
                own[32 + (big_i * 2 + big_j) * 4 + t] = upper[:, t * 128 : (t + 1) * 128]
    uppers = own.at[pl.ds(32, 16)]
    for target, at in ((up_hbm, 12), (down_hbm, 12), (own_hbm, 32)):
        send(uppers, target.at[pl.ds(at, 16)])
    for copy in sent:
        copy.wait()


def pass_kernel(pieces, same):
    del pieces, same


def pack_kernel(own, before, after, right, left):
    for target, col in ((right, 2), (left, 0)):
        edge_col = 3 if col else 0
        moves = [
            (before, col * 2, 0, 4),
            (own, col * 4, 4, 8),
            (after, col * 2, 12, 4),
            (before, 8 + edge_col, 16, 1),
            (own, 16 + edge_col * 4, 17, 4),
            (after, 8 + edge_col, 21, 1),
            (before, 12, 22, 16),
            (own, 32, 38, 16),
            (after, 12, 54, 16),
        ]
        for source, start, at, size in moves:
            target[at : at + size] = source[start : start + size]


def near_sum(masks, real_blocks, imag_blocks):
    row = jnp.concatenate(masks, axis=1)
    first = dot_nt(row, jnp.concatenate(real_blocks, axis=1))
    second = dot_nt(row, jnp.concatenate(imag_blocks, axis=1))
    return pair(first[0:8] - second[8:16], first[8:16] + second[0:8])


def masked_unit(unit, flag):
    return (unit.astype(F32) * flag).astype(BF16)


def inside(j):
    return [dy for dy in (-1, 0, 1) if 0 <= j + dy < 4]


def near_kernel(own, before, after, blocks, out, rest, held, sems, rest_sems):
    copies = []
    for i in range(4):
        group = [pltpu.make_async_copy(blocks.at[:, i, 1:3], held.at[:, i, 1:3], sems.at[i, 0])]
        for j, low in ((0, 1), (3, 0)):
            for dx in range(3):
                span = pl.ds(3 * dx + low, 2)
                group.append(
                    pltpu.make_async_copy(
                        blocks.at[:, i, j, span], held.at[:, i, j, span], sems.at[i, len(group)]
                    )
                )
        copies.append(group)
    for group in copies:
        for copy in group:
            copy.start()
    rest_copies = []
    for side, j in enumerate((0, 3)):
        for dx in range(3):
            slot = side * 3 + dx
            rest_copies.append(
                pltpu.make_async_copy(
                    blocks.at[:, :, j, 3 * dx + 2 * side], rest.at[slot], rest_sems.at[slot]
                )
            )
    for copy in rest_copies:
        copy.start()
    here = lax.axis_index("box")
    has_before = (here > 0).astype(F32)
    has_after = (here < lax.axis_size("box") - 1).astype(F32)
    rows = {}
    for j in range(4):
        rows[-1, j] = (before[8 + j].astype(F32) * has_before).astype(BF16)
        rows[4, j] = (after[8 + j].astype(F32) * has_after).astype(BF16)
        for i in range(4):
            rows[i, j] = own[16 + j * 4 + i]
    for i in range(4):
        for copy in copies[i]:
            copy.wait()
        for j in range(4):
            pairs = [(dx, dy) for dx in (-1, 0, 1) for dy in inside(j)]
            out[i * 4 + j] = near_sum(
                [rows[i + dx, j + dy] for dx, dy in pairs],
                [held[0, i, j, 3 * (dx + 1) + dy + 1] for dx, dy in pairs],
                [held[1, i, j, 3 * (dx + 1) + dy + 1] for dx, dy in pairs],
            )
    for copy in rest_copies:
        copy.wait()


def translate(source, coef, keep):
    total = {}
    for r in range(6):
        for c in range(6):
            unit = source(r, c)
            s_re, s_im = unit[0:8], unit[8:16]
            for a in range(2):
                for b in range(2):
                    dx, dy = r - 2 - a, c - 2 - b
                    if max(abs(dx), abs(dy)) < 2:
                        continue
                    k_re, k_im = coef(0, dx, dy), coef(1, dx, dy)
                    t_re = k_re * s_re - k_im * s_im
                    t_im = k_re * s_im + k_im * s_re
                    if (a, b) in total:
                        old_re, old_im = total[a, b]
                        t_re, t_im = old_re + t_re, old_im + t_im
                    total[a, b] = (t_re, t_im)
    for (a, b), (t_re, t_im) in total.items():
        keep(a, b, pair(t_re, t_im))


def middle_kernel(
    own,
    before,
    after,
    left,
    right,
    trans_leaf,
    near,
    rest,
    far,
    upper_halo,
    field,
    leaf_halo,
):
    box, col = lax.axis_index("box"), lax.axis_index("dir")
    f_before = (box > 0).astype(F32)
    f_after = (box < lax.axis_size("box") - 1).astype(F32)
    f_left = (col > 0).astype(F32)
    f_right = (col < lax.axis_size("dir") - 1).astype(F32)

    for j in range(4):
        for r in range(2):
            leaf_halo[r * 8 + j + 2] = before[j * 2 + r].astype(F32) * f_before
            leaf_halo[(r + 6) * 8 + j + 2] = after[j * 2 + r].astype(F32) * f_after
        for i in range(4):
            leaf_halo[(i + 2) * 8 + j + 2] = own[j * 4 + i].astype(F32)
    for part, flag, start in ((left, f_left, 0), (right, f_right, 6)):
        for c in range(2):
            for r in range(2):
                leaf_halo[r * 8 + start + c] = part[c * 2 + r].astype(F32) * (flag * f_before)
                leaf_halo[(r + 6) * 8 + start + c] = part[12 + c * 2 + r].astype(F32) * (
                    flag * f_after
                )
            for i in range(4):
                leaf_halo[(i + 2) * 8 + start + c] = part[4 + c * 4 + i].astype(F32) * flag
    for p in range(2):
        for q in range(2):
            for t in range(4):
                unit = (p * 2 + q) * 4 + t
                upper_halo[t, p * 6 + q + 2] = masked_unit(before[12 + unit], f_before)
                upper_halo[t, (p + 2) * 6 + q + 2] = own[32 + unit]
                upper_halo[t, (p + 4) * 6 + q + 2] = masked_unit(after[12 + unit], f_after)
                for part, flag, start in ((left, f_left, 0), (right, f_right, 4)):
                    upper_halo[t, p * 6 + q + start] = masked_unit(
                        part[22 + unit], flag * f_before
                    )
                    upper_halo[t, (p + 2) * 6 + q + start] = masked_unit(part[38 + unit], flag)
                    upper_halo[t, (p + 4) * 6 + q + start] = masked_unit(
                        part[54 + unit], flag * f_after
                    )

    def leaf_step(quad, carry):
        base = (quad // 2) * 16 + (quad % 2) * 2

        def keep(a, b, value):
            far[quad * 4 + a * 2 + b] = value

        translate(
            lambda r, c: leaf_halo[base + r * 8 + c],
            lambda part, dx, dy: trans_leaf[dx + 3, dy + 3, pl.ds(part, 1), :],
            keep,
        )
        return carry

    lax.fori_loop(0, 4, leaf_step, 0)

    sides = {}
    for j, part, flag in ((0, left, f_left), (3, right, f_right)):
        sides[j, -1] = masked_unit(part[16], flag * f_before)
        sides[j, 4] = masked_unit(part[21], flag * f_after)
        for i in range(4):
            sides[j, i] = masked_unit(part[17 + i], flag)
    for i in range(4):
        for j in range(4):
            value = near[i * 4 + j]
            if j in (0, 3):
                slots = [(3 if j else 0) + dx for dx in range(3)]
                value = value + near_sum(
                    [sides[j, i + dx] for dx in (-1, 0, 1)],
                    [rest[slot, 0, i] for slot in slots],
                    [rest[slot, 1, i] for slot in slots],
                )
            field[i * 4 + j] = value


def final_kernel(
    live,
    upper_halo,
    pieces,
    far,
    anterp,
    phase,
    near,
    rad,
    out_hbm,
    out,
    table,
    top,
    out_sems,
):
    for t in range(4):
        table[t] = pieces[pl.ds(t * 32, 32)].astype(F32).reshape(128, 128).T

    def top_step(t, carry):
        def keep(a, b, value):
            top[t, a * 2 + b] = value.astype(BF16).astype(F32)

        translate(
            lambda r, c: upper_halo[t, r * 6 + c].astype(F32),
            lambda part, dx, dy: table[t, pl.ds((part * 7 + dx + 3) * 8 + dy + 3, 1), :],
            keep,
        )
        return carry

    lax.fori_loop(0, 4, top_step, 0)

    rows = []
    for quad in range(4):
        for child in range(4):
            tiles = []
            for t in range(4):
                unit = top[t, quad]
                t_re, t_im = unit[0:8], unit[8:16]
                c = phase[child : child + 1, t * 128 : (t + 1) * 128]
                s = phase[4 + child : 5 + child, t * 128 : (t + 1) * 128]
                tiles.append(pair(c * t_re + s * t_im, c * t_im - s * t_re).astype(BF16))
            rows.append(jnp.concatenate(tiles, axis=1))
    back = dot_nt(jnp.concatenate(rows, axis=0), anterp[...])
    sent = []
    for i in range(4):
        for j in range(4):
            at = ((i // 2) * 2 + j // 2) * 4 + (i % 2) * 2 + j % 2
            total = (far[at] + back[at * 16 : at * 16 + 16]).astype(BF16)
            both = dot_nt(total, rad[:, i, j].reshape(256, 128))
            first, second = both[:, 0:128], both[:, 128:256]
            field = near[i * 4 + j] + pair(
                first[0:8] + second[8:16], first[8:16] - second[0:8]
            )
            on = live[i * 4 + j]
            out[0, i, j] = field[0:8] * on
            out[1, i, j] = field[8:16] * on
        sent.append(pltpu.make_async_copy(out.at[:, i], out_hbm.at[:, i], out_sems.at[i]))
        sent[-1].start()
    for copy in sent:
        copy.wait()


def unit_shape(count):
    return jax.ShapeDtypeStruct((count, 16, 128), BF16)


def shards(
    coeffs, counts, radiation, near_blocks, trans_leaf, interp, anterp, shift_angle, trans_top
):
    n_box = lax.axis_size("box")
    n_dir = lax.axis_size("dir")
    devices = n_box * n_dir
    outputs = (
        unit_shape(OWN),
        unit_shape(EDGE),
        unit_shape(EDGE),
        jax.ShapeDtypeStruct((8, 512), F32),
        jax.ShapeDtypeStruct((16, 8, 128), F32),
        jax.ShapeDtypeStruct((devices, 4, 128), F32),
    )
    own, to_after, to_before, phase, live, pieces = pl.pallas_call(
        leaf_kernel,
        out_shape=outputs,
        in_specs=[hbm()] * 6,
        out_specs=(hbm(),) * 6,
        scratch_shapes=[
            pltpu.SMEM((4, 4), jnp.int32),
            pltpu.VMEM((2, 4, 4, 8, 128), BF16),
            pltpu.VMEM((2, 4, 4, 128, 128), BF16),
            pltpu.VMEM((512, 128), BF16),
            pltpu.VMEM((4, 512), F32),
            pltpu.VMEM((2, 7, 4, 7), F32),
        ]
        + [pltpu.VMEM(out.shape, out.dtype) for out in outputs]
        + [
            pltpu.SemaphoreType.DMA((5,)),
            pltpu.SemaphoreType.DMA((4,)),
            pltpu.SemaphoreType.DMA((9,)),
        ],
        compiler_params=params(62),
        cost_estimate=cost(2),
        name="leaf",
    )(counts, coeffs, radiation, interp, shift_angle, trans_top.transpose(0, 1, 3, 2))
    forward = [(i, (i + 1) % n_box) for i in range(n_box)]
    backward = [((i + 1) % n_box, i) for i in range(n_box)]
    before = lax.ppermute(to_after, "box", forward)
    after = lax.ppermute(to_before, "box", backward)
    pieces = pl.pallas_call(
        pass_kernel,
        out_shape=jax.ShapeDtypeStruct((devices, 4, 128), F32),
        in_specs=[hbm()],
        out_specs=hbm(),
        input_output_aliases={0: 0},
        compiler_params=params(62),
        cost_estimate=cost(20),
        name="pass",
    )(pieces)
    gathered = lax.all_to_all(pieces, ("box", "dir"), split_axis=0, concat_axis=0, tiled=True)
    to_right, to_left = pl.pallas_call(
        pack_kernel,
        out_shape=(unit_shape(SIDE), unit_shape(SIDE)),
        in_specs=[vmem()] * 3,
        out_specs=(vmem(),) * 2,
        compiler_params=params(4),
        cost_estimate=cost(20),
        name="pack",
    )(own, before, after)
    left = lax.ppermute(to_right, "dir", [(i, (i + 1) % n_dir) for i in range(n_dir)])
    right = lax.ppermute(to_left, "dir", [((i + 1) % n_dir, i) for i in range(n_dir)])
    near, rest = pl.pallas_call(
        near_kernel,
        out_shape=(
            jax.ShapeDtypeStruct((16, 16, 128), F32),
            jax.ShapeDtypeStruct((6, 2, 4, 128, 128), BF16),
        ),
        in_specs=[vmem()] * 3 + [hbm()],
        out_specs=(vmem(),) * 2,
        scratch_shapes=[
            pltpu.VMEM((2, 4, 4, 9, 128, 128), BF16),
            pltpu.SemaphoreType.DMA((4, 7)),
            pltpu.SemaphoreType.DMA((6,)),
        ],
        compiler_params=params(48),
        cost_estimate=cost(4),
        name="near",
    )(own, before, after, near_blocks)
    far, upper_halo, near = pl.pallas_call(
        middle_kernel,
        out_shape=(
            jax.ShapeDtypeStruct((16, 16, 128), F32),
            jax.ShapeDtypeStruct((4, 36, 16, 128), BF16),
            jax.ShapeDtypeStruct((16, 16, 128), F32),
        ),
        in_specs=[vmem()] * 8,
        out_specs=(vmem(),) * 3,
        scratch_shapes=[pltpu.VMEM((64, 16, 128), F32)],
        compiler_params=params(48),
        cost_estimate=cost(2),
        name="middle",
    )(
        own,
        before,
        after,
        left,
        right,
        trans_leaf.transpose(1, 2, 0, 3),
        near,
        rest,
    )
    return pl.pallas_call(
        final_kernel,
        out_shape=jax.ShapeDtypeStruct((2, 4, 4, 8, 128), F32),
        in_specs=[vmem()] * 8,
        out_specs=hbm(),
        scratch_shapes=[
            pltpu.VMEM((2, 4, 4, 8, 128), F32),
            pltpu.VMEM((4, 128, 128), F32),
            pltpu.VMEM((4, 4, 16, 128), F32),
            pltpu.SemaphoreType.DMA((4,)),
        ],
        compiler_params=params(48),
        cost_estimate=cost(4),
        name="final",
    )(live, upper_halo, gathered, far, anterp, phase, near, radiation)


def solution(mesh):
    return jax.shard_map(
        shards,
        mesh=mesh,
        in_specs=(
            P(None, "box", "dir", None, None),
            P("box", "dir"),
            P(None, "box", "dir", None, None),
            P(None, "box", "dir", None, None, None),
            P(),
            P(),
            P(),
            P(),
            P(None, None, None, ("box", "dir")),
        ),
        out_specs=P(None, "box", "dir", None, None),
        check_vma=False,
    )
```

```python
import jax
import jax.numpy as jnp
from jax import lax
from jax.experimental import pallas as pl
from jax.experimental.pallas import tpu as pltpu
from jax.sharding import PartitionSpec as P

OWN, EDGE, SIDE = 48, 28, 70
NT = (((1,), (1,)), ((), ()))
F32 = jnp.float32
BF16 = jnp.bfloat16


def dot_nt(left, right):
    return lax.dot_general(left, right, NT, preferred_element_type=F32)


def pair(real, imag):
    return jnp.concatenate([real, imag], axis=0)


def vmem():
    return pl.BlockSpec(memory_space=pltpu.VMEM)


def hbm():
    return pl.BlockSpec(memory_space=pl.ANY)


def params(mib):
    return pltpu.CompilerParams(vmem_limit_bytes=mib << 20)


def cost(us):
    return pl.CostEstimate(flops=us * 10**9, bytes_accessed=us << 20, transcendentals=0)


def leaf_kernel(
    counts_hbm,
    coeffs_hbm,
    radiation,
    interp_hbm,
    angle_hbm,
    table_hbm,
    own_hbm,
    up_hbm,
    down_hbm,
    phase_hbm,
    live_hbm,
    pieces_hbm,
    counts,
    coeffs,
    rad,
    interp,
    angle,
    table,
    own,
    up,
    down,
    phase,
    live,
    pieces,
    sems,
    rad_sems,
    out_sems,
):
    counts_in = pltpu.make_async_copy(counts_hbm, counts, sems.at[0])
    coeffs_in = pltpu.make_async_copy(coeffs_hbm, coeffs, sems.at[1])
    angle_in = pltpu.make_async_copy(angle_hbm, angle, sems.at[2])
    table_in = pltpu.make_async_copy(table_hbm, table, sems.at[3])
    interp_in = pltpu.make_async_copy(interp_hbm, interp, sems.at[4])
    rad_in = [
        pltpu.make_async_copy(radiation.at[:, i], rad.at[:, i], rad_sems.at[i]) for i in range(4)
    ]
    for copy in (table_in, angle_in, counts_in, coeffs_in, *rad_in, interp_in):
        copy.start()
    sent = []

    def send(source, target):
        copy = pltpu.make_async_copy(source, target, out_sems.at[len(sent)])
        copy.start()
        sent.append(copy)

    pieces[0] = jnp.zeros((4, 128), BF16)
    table_in.wait()
    for part in range(2):
        for dx in range(7):
            at = (part * 7 + dx) * 8
            pieces[0, :, at : at + 7] = table[part, dx].astype(BF16)
    pieces[...] = jnp.broadcast_to(pieces[0:1], pieces.shape)
    send(pieces, pieces_hbm)
    angle_in.wait()
    cosine = jnp.cos(angle[...])
    sine = jnp.sin(angle[...])
    phase[0:4, :] = cosine
    phase[4:8, :] = sine
    send(phase, phase_hbm)
    counts_in.wait()
    lane = lax.broadcasted_iota(jnp.int32, (8, 128), 1)
    for i in range(4):
        for j in range(4):
            live[i * 4 + j] = (lane < counts[i, j]).astype(F32)
    send(live, live_hbm)
    coeffs_in.wait()
    for copy in rad_in:
        copy.wait()
    leaves = []
    for i in range(4):
        for j in range(4):
            on = live[i * 4 + j]
            masked = pair(
                coeffs[0, i, j].astype(F32) * on, coeffs[1, i, j].astype(F32) * on
            ).astype(BF16)
            wide = jnp.concatenate([rad[0, i, j], rad[1, i, j]], axis=1)
            prod = jnp.dot(masked, wide, preferred_element_type=F32)
            first, second = prod[:, 0:128], prod[:, 128:256]
            leaf = pair(first[0:8] - second[8:16], first[8:16] + second[0:8]).astype(BF16)
            leaves.append(leaf)
            own[j * 4 + i] = leaf
            own[16 + j * 4 + i] = masked
            if i < 2:
                down[j * 2 + i] = leaf
            else:
                up[j * 2 + i - 2] = leaf
            if i == 0:
                down[8 + j] = masked
            if i == 3:
                up[8 + j] = masked
    for source, target, count in ((up, up_hbm, 12), (down, down_hbm, 12), (own, own_hbm, 32)):
        send(source.at[pl.ds(0, count)], target.at[pl.ds(0, count)])
    interp_in.wait()
    spread = dot_nt(jnp.concatenate(leaves, axis=0), interp[...])
    for big_i in range(2):
        for big_j in range(2):
            real = imag = None
            for a in range(2):
                for b in range(2):
                    at = ((2 * big_i + a) * 4 + 2 * big_j + b) * 16
                    s_re, s_im = spread[at : at + 8], spread[at + 8 : at + 16]
                    c = cosine[2 * a + b : 2 * a + b + 1]
                    s = sine[2 * a + b : 2 * a + b + 1]
                    t_re = c * s_re - s * s_im
                    t_im = c * s_im + s * s_re
                    real = t_re if real is None else real + t_re
                    imag = t_im if imag is None else imag + t_im
            upper = pair(real, imag).astype(BF16)
            for t in range(4):
                own[32 + (big_i * 2 + big_j) * 4 + t] = upper[:, t * 128 : (t + 1) * 128]
    uppers = own.at[pl.ds(32, 16)]
    for target, at in ((up_hbm, 12), (down_hbm, 12), (own_hbm, 32)):
        send(uppers, target.at[pl.ds(at, 16)])
    for copy in sent:
        copy.wait()


def pass_kernel(pieces, same):
    del pieces, same


def pack_kernel(own, before, after, right, left):
    for target, col in ((right, 2), (left, 0)):
        edge_col = 3 if col else 0
        moves = [
            (before, col * 2, 0, 4),
            (own, col * 4, 4, 8),
            (after, col * 2, 12, 4),
            (before, 8 + edge_col, 16, 1),
            (own, 16 + edge_col * 4, 17, 4),
            (after, 8 + edge_col, 21, 1),
            (before, 12, 22, 16),
            (own, 32, 38, 16),
            (after, 12, 54, 16),
        ]
        for source, start, at, size in moves:
            target[at : at + size] = source[start : start + size]


def near_sum(masks, real_blocks, imag_blocks):
    row = jnp.concatenate(masks, axis=1)
    first = dot_nt(row, jnp.concatenate(real_blocks, axis=1))
    second = dot_nt(row, jnp.concatenate(imag_blocks, axis=1))
    return pair(first[0:8] - second[8:16], first[8:16] + second[0:8])


def border_flags():
    box, col = lax.axis_index("box"), lax.axis_index("dir")
    return (
        (box > 0).astype(F32),
        (box < lax.axis_size("box") - 1).astype(F32),
        (col > 0).astype(F32),
        (col < lax.axis_size("dir") - 1).astype(F32),
    )


def masked_unit(unit, flag):
    return (unit.astype(F32) * flag).astype(BF16)


def inside(j):
    return [dy for dy in (-1, 0, 1) if 0 <= j + dy < 4]


def near_kernel(
    own, before, after, trans_leaf, blocks, out, rest, far, held, leaf_halo, sems, rest_sems
):
    copies = []
    for i in range(4):
        group = [pltpu.make_async_copy(blocks.at[:, i, 1:3], held.at[:, i, 1:3], sems.at[i, 0])]
        for j, low in ((0, 1), (3, 0)):
            for dx in range(3):
                span = pl.ds(3 * dx + low, 2)
                group.append(
                    pltpu.make_async_copy(
                        blocks.at[:, i, j, span], held.at[:, i, j, span], sems.at[i, len(group)]
                    )
                )
        copies.append(group)
    for group in copies:
        for copy in group:
            copy.start()
    rest_copies = []
    for side, j in enumerate((0, 3)):
        for dx in range(3):
            slot = side * 3 + dx
            rest_copies.append(
                pltpu.make_async_copy(
                    blocks.at[:, :, j, 3 * dx + 2 * side], rest.at[slot], rest_sems.at[slot]
                )
            )
    for copy in rest_copies:
        copy.start()
    has_before, has_after, _, _ = border_flags()
    rows = {}
    for j in range(4):
        rows[-1, j] = (before[8 + j].astype(F32) * has_before).astype(BF16)
        rows[4, j] = (after[8 + j].astype(F32) * has_after).astype(BF16)
        for i in range(4):
            rows[i, j] = own[16 + j * 4 + i]
    for j in range(4):
        for r in range(2):
            leaf_halo[r * 4 + j] = before[j * 2 + r].astype(F32) * has_before
            leaf_halo[(r + 6) * 4 + j] = after[j * 2 + r].astype(F32) * has_after
        for i in range(4):
            leaf_halo[(i + 2) * 4 + j] = own[j * 4 + i].astype(F32)

    def far_step(big_i, carry):
        for big_j in range(2):
            first = 2 - 2 * big_j
            total = translate(
                lambda r, c: leaf_halo[(big_i * 2 + r) * 4 + c - first],
                lambda part, dx, dy: trans_leaf[dx + 3, dy + 3, pl.ds(part, 1), :],
                {},
                range(first, first + 4),
            )
            for a, b in CHILDREN:
                far[(big_i * 2 + big_j) * 4 + a * 2 + b] = pair(*total[a, b])
        return carry

    lax.fori_loop(0, 2, far_step, 0)
    for i in range(4):
        for copy in copies[i]:
            copy.wait()
        for j in range(4):
            pairs = [(dx, dy) for dx in (-1, 0, 1) for dy in inside(j)]
            out[i * 4 + j] = near_sum(
                [rows[i + dx, j + dy] for dx, dy in pairs],
                [held[0, i, j, 3 * (dx + 1) + dy + 1] for dx, dy in pairs],
                [held[1, i, j, 3 * (dx + 1) + dy + 1] for dx, dy in pairs],
            )
    for copy in rest_copies:
        copy.wait()


def translate(source, coef, start, cols):
    total = dict(start)
    for dx in range(-3, 4):
        for dy in range(-3, 4):
            if max(abs(dx), abs(dy)) < 2:
                continue
            k_re = k_im = None
            for a in range(2):
                for b in range(2):
                    r, c = dx + 2 + a, dy + 2 + b
                    if not 0 <= r < 6 or c not in cols:
                        continue
                    if k_re is None:
                        k_re = jnp.broadcast_to(coef(0, dx, dy), (8, 128))
                        k_im = jnp.broadcast_to(coef(1, dx, dy), (8, 128))
                    unit = source(r, c)
                    s_re, s_im = unit[0:8], unit[8:16]
                    t_re = k_re * s_re - k_im * s_im
                    t_im = k_re * s_im + k_im * s_re
                    if (a, b) in total:
                        old_re, old_im = total[a, b]
                        t_re, t_im = old_re + t_re, old_im + t_im
                    total[a, b] = (t_re, t_im)
    return total


CHILDREN = [(a, b) for a in range(2) for b in range(2)]


def middle_kernel(
    own,
    before,
    after,
    left,
    right,
    trans_leaf,
    near,
    rest,
    far_own,
    far,
    upper_halo,
    field,
    leaf_halo,
):
    f_before, f_after, f_left, f_right = border_flags()
    for side, (part, flag) in enumerate(((left, f_left), (right, f_right))):
        for c in range(2):
            for r in range(2):
                leaf_halo[side, r * 2 + c] = part[c * 2 + r].astype(F32) * (flag * f_before)
                leaf_halo[side, (r + 6) * 2 + c] = part[12 + c * 2 + r].astype(F32) * (
                    flag * f_after
                )
            for i in range(4):
                leaf_halo[side, (i + 2) * 2 + c] = part[4 + c * 4 + i].astype(F32) * flag
    for p in range(2):
        for q in range(2):
            for t in range(4):
                unit = (p * 2 + q) * 4 + t
                upper_halo[t, p * 6 + q + 2] = before[12 + unit].astype(F32) * f_before
                upper_halo[t, (p + 2) * 6 + q + 2] = own[32 + unit].astype(F32)
                upper_halo[t, (p + 4) * 6 + q + 2] = after[12 + unit].astype(F32) * f_after
                for part, flag, start in ((left, f_left, 0), (right, f_right, 4)):
                    upper_halo[t, p * 6 + q + start] = part[22 + unit].astype(F32) * (
                        flag * f_before
                    )
                    upper_halo[t, (p + 2) * 6 + q + start] = part[38 + unit].astype(F32) * flag
                    upper_halo[t, (p + 4) * 6 + q + start] = part[54 + unit].astype(F32) * (
                        flag * f_after
                    )

    def far_step(big_i, carry):
        for big_j in range(2):
            first = 4 * big_j
            at = (big_i * 2 + big_j) * 4
            start = {}
            for a, b in CHILDREN:
                unit = far_own[at + a * 2 + b]
                start[a, b] = (unit[0:8], unit[8:16])
            total = translate(
                lambda r, c: leaf_halo[big_j, (big_i * 2 + r) * 2 + c - first],
                lambda part, dx, dy: trans_leaf[dx + 3, dy + 3, pl.ds(part, 1), :],
                start,
                range(first, first + 2),
            )
            for a, b in CHILDREN:
                far[at + a * 2 + b] = pair(*total[a, b])
        return carry

    lax.fori_loop(0, 2, far_step, 0)

    sides = {}
    for j, part, flag in ((0, left, f_left), (3, right, f_right)):
        sides[j, -1] = masked_unit(part[16], flag * f_before)
        sides[j, 4] = masked_unit(part[21], flag * f_after)
        for i in range(4):
            sides[j, i] = masked_unit(part[17 + i], flag)
    for i in range(4):
        for j in range(4):
            value = near[i * 4 + j]
            if j in (0, 3):
                slots = [(3 if j else 0) + dx for dx in range(3)]
                value = value + near_sum(
                    [sides[j, i + dx] for dx in (-1, 0, 1)],
                    [rest[slot, 0, i] for slot in slots],
                    [rest[slot, 1, i] for slot in slots],
                )
            field[i * 4 + j] = value


def final_kernel(
    live,
    upper_halo,
    pieces,
    far,
    anterp,
    phase,
    near,
    rad,
    out_hbm,
    out,
    table,
    top,
    out_sems,
):
    for t in range(4):
        table[t] = pieces[pl.ds(t * 32, 32)].astype(F32).reshape(128, 128).T

    def top_step(t, carry):
        total = translate(
            lambda r, c: upper_halo[t, r * 6 + c],
            lambda part, dx, dy: table[t, pl.ds((part * 7 + dx + 3) * 8 + dy + 3, 1), :],
            {},
            range(6),
        )
        for a, b in CHILDREN:
            top[t, a * 2 + b] = pair(*total[a, b]).astype(BF16).astype(F32)
        return carry

    lax.fori_loop(0, 4, top_step, 0)

    rows = []
    for quad in range(4):
        for child in range(4):
            tiles = []
            for t in range(4):
                unit = top[t, quad]
                t_re, t_im = unit[0:8], unit[8:16]
                c = phase[child : child + 1, t * 128 : (t + 1) * 128]
                s = phase[4 + child : 5 + child, t * 128 : (t + 1) * 128]
                tiles.append(pair(c * t_re + s * t_im, c * t_im - s * t_re).astype(BF16))
            rows.append(jnp.concatenate(tiles, axis=1))
    back = dot_nt(jnp.concatenate(rows, axis=0), anterp[...])
    sent = []
    for i in range(4):
        for j in range(4):
            at = ((i // 2) * 2 + j // 2) * 4 + (i % 2) * 2 + j % 2
            total = (far[at] + back[at * 16 : at * 16 + 16]).astype(BF16)
            both = dot_nt(total, rad[:, i, j].reshape(256, 128))
            first, second = both[:, 0:128], both[:, 128:256]
            field = near[i * 4 + j] + pair(
                first[0:8] + second[8:16], first[8:16] - second[0:8]
            )
            on = live[i * 4 + j]
            out[0, i, j] = field[0:8] * on
            out[1, i, j] = field[8:16] * on
        sent.append(pltpu.make_async_copy(out.at[:, i], out_hbm.at[:, i], out_sems.at[i]))
        sent[-1].start()
    for copy in sent:
        copy.wait()


def unit_shape(count):
    return jax.ShapeDtypeStruct((count, 16, 128), BF16)


def shards(
    coeffs, counts, radiation, near_blocks, trans_leaf, interp, anterp, shift_angle, trans_top
):
    n_box = lax.axis_size("box")
    n_dir = lax.axis_size("dir")
    devices = n_box * n_dir
    outputs = (
        unit_shape(OWN),
        unit_shape(EDGE),
        unit_shape(EDGE),
        jax.ShapeDtypeStruct((8, 512), F32),
        jax.ShapeDtypeStruct((16, 8, 128), F32),
        jax.ShapeDtypeStruct((devices, 4, 128), BF16),
    )
    own, to_after, to_before, phase, live, pieces = pl.pallas_call(
        leaf_kernel,
        out_shape=outputs,
        in_specs=[hbm()] * 6,
        out_specs=(hbm(),) * 6,
        scratch_shapes=[
            pltpu.SMEM((4, 4), jnp.int32),
            pltpu.VMEM((2, 4, 4, 8, 128), BF16),
            pltpu.VMEM((2, 4, 4, 128, 128), BF16),
            pltpu.VMEM((512, 128), BF16),
            pltpu.VMEM((4, 512), F32),
            pltpu.VMEM((2, 7, 4, 7), F32),
        ]
        + [pltpu.VMEM(out.shape, out.dtype) for out in outputs]
        + [
            pltpu.SemaphoreType.DMA((5,)),
            pltpu.SemaphoreType.DMA((4,)),
            pltpu.SemaphoreType.DMA((9,)),
        ],
        compiler_params=params(62),
        cost_estimate=cost(2),
        name="leaf",
    )(counts, coeffs, radiation, interp, shift_angle, trans_top.transpose(0, 1, 3, 2))
    forward = [(i, (i + 1) % n_box) for i in range(n_box)]
    backward = [((i + 1) % n_box, i) for i in range(n_box)]
    before = lax.ppermute(to_after, "box", forward)
    after = lax.ppermute(to_before, "box", backward)
    pieces = pl.pallas_call(
        pass_kernel,
        out_shape=jax.ShapeDtypeStruct((devices, 4, 128), BF16),
        in_specs=[hbm()],
        out_specs=hbm(),
        input_output_aliases={0: 0},
        compiler_params=params(62),
        cost_estimate=cost(20),
        name="pass",
    )(pieces)
    gathered = lax.all_to_all(pieces, ("box", "dir"), split_axis=0, concat_axis=0, tiled=True)
    to_right, to_left = pl.pallas_call(
        pack_kernel,
        out_shape=(unit_shape(SIDE), unit_shape(SIDE)),
        in_specs=[vmem()] * 3,
        out_specs=(vmem(),) * 2,
        compiler_params=params(4),
        cost_estimate=cost(20),
        name="pack",
    )(own, before, after)
    left = lax.ppermute(to_right, "dir", [(i, (i + 1) % n_dir) for i in range(n_dir)])
    right = lax.ppermute(to_left, "dir", [((i + 1) % n_dir, i) for i in range(n_dir)])
    by_offset = trans_leaf.transpose(1, 2, 0, 3)
    near, rest, far = pl.pallas_call(
        near_kernel,
        out_shape=(
            jax.ShapeDtypeStruct((16, 16, 128), F32),
            jax.ShapeDtypeStruct((6, 2, 4, 128, 128), BF16),
            jax.ShapeDtypeStruct((16, 16, 128), F32),
        ),
        in_specs=[vmem()] * 4 + [hbm()],
        out_specs=(vmem(),) * 3,
        scratch_shapes=[
            pltpu.VMEM((2, 4, 4, 9, 128, 128), BF16),
            pltpu.VMEM((32, 16, 128), F32),
            pltpu.SemaphoreType.DMA((4, 7)),
            pltpu.SemaphoreType.DMA((6,)),
        ],
        compiler_params=params(48),
        cost_estimate=cost(4),
        name="near",
    )(own, before, after, by_offset, near_blocks)
    far, upper_halo, near = pl.pallas_call(
        middle_kernel,
        out_shape=(
            jax.ShapeDtypeStruct((16, 16, 128), F32),
            jax.ShapeDtypeStruct((4, 36, 16, 128), F32),
            jax.ShapeDtypeStruct((16, 16, 128), F32),
        ),
        in_specs=[vmem()] * 9,
        out_specs=(vmem(),) * 3,
        scratch_shapes=[pltpu.VMEM((2, 16, 16, 128), F32)],
        compiler_params=params(48),
        cost_estimate=cost(2),
        name="middle",
    )(own, before, after, left, right, by_offset, near, rest, far)
    return pl.pallas_call(
        final_kernel,
        out_shape=jax.ShapeDtypeStruct((2, 4, 4, 8, 128), F32),
        in_specs=[vmem()] * 8,
        out_specs=hbm(),
        scratch_shapes=[
            pltpu.VMEM((2, 4, 4, 8, 128), F32),
            pltpu.VMEM((4, 128, 128), F32),
            pltpu.VMEM((4, 4, 16, 128), F32),
            pltpu.SemaphoreType.DMA((4,)),
        ],
        compiler_params=params(48),
        cost_estimate=cost(4),
        name="final",
    )(live, upper_halo, gathered, far, anterp, phase, near, radiation)


def solution(mesh):
    return jax.shard_map(
        shards,
        mesh=mesh,
        in_specs=(
            P(None, "box", "dir", None, None),
            P("box", "dir"),
            P(None, "box", "dir", None, None),
            P(None, "box", "dir", None, None, None),
            P(),
            P(),
            P(),
            P(),
            P(None, None, None, ("box", "dir")),
        ),
        out_specs=P(None, "box", "dir", None, None),
        check_vma=False,
    )
```

```python
import jax
import jax.numpy as jnp
from jax import lax
from jax.experimental import pallas as pl
from jax.experimental.pallas import tpu as pltpu
from jax.sharding import PartitionSpec as P

OWN, EDGE, SIDE = 48, 28, 70
NT = (((1,), (1,)), ((), ()))
F32 = jnp.float32
BF16 = jnp.bfloat16


def dot_nt(left, right):
    return lax.dot_general(left, right, NT, preferred_element_type=F32)


def pair(real, imag):
    return jnp.concatenate([real, imag], axis=0)


def vmem():
    return pl.BlockSpec(memory_space=pltpu.VMEM)


def hbm():
    return pl.BlockSpec(memory_space=pl.ANY)


def params(mib):
    return pltpu.CompilerParams(vmem_limit_bytes=mib << 20)


def cost(us):
    return pl.CostEstimate(flops=us * 10**9, bytes_accessed=us << 20, transcendentals=0)


def leaf_kernel(
    counts_hbm,
    coeffs_hbm,
    radiation,
    interp_hbm,
    angle_hbm,
    table_hbm,
    own_hbm,
    up_hbm,
    down_hbm,
    phase_hbm,
    live_hbm,
    pieces_hbm,
    counts,
    coeffs,
    rad,
    interp,
    angle,
    table,
    own,
    up,
    down,
    phase,
    live,
    pieces,
    sems,
    rad_sems,
    out_sems,
):
    counts_in = pltpu.make_async_copy(counts_hbm, counts, sems.at[0])
    coeffs_in = pltpu.make_async_copy(coeffs_hbm, coeffs, sems.at[1])
    angle_in = pltpu.make_async_copy(angle_hbm, angle, sems.at[2])
    table_in = pltpu.make_async_copy(table_hbm, table, sems.at[3])
    interp_in = pltpu.make_async_copy(interp_hbm, interp, sems.at[4])
    rad_in = [
        pltpu.make_async_copy(radiation.at[:, i], rad.at[:, i], rad_sems.at[i]) for i in range(4)
    ]
    for copy in (table_in, angle_in, counts_in, coeffs_in, *rad_in, interp_in):
        copy.start()
    sent = []

    def send(source, target):
        copy = pltpu.make_async_copy(source, target, out_sems.at[len(sent)])
        copy.start()
        sent.append(copy)

    pieces[0] = jnp.zeros((4, 128), BF16)
    table_in.wait()
    for part in range(2):
        for dx in range(7):
            at = (part * 7 + dx) * 8
            pieces[0, :, at : at + 7] = table[part, dx].astype(BF16)
    pieces[...] = jnp.broadcast_to(pieces[0:1], pieces.shape)
    send(pieces, pieces_hbm)
    angle_in.wait()
    cosine = jnp.cos(angle[...])
    sine = jnp.sin(angle[...])
    phase[0:4, :] = cosine
    phase[4:8, :] = sine
    send(phase, phase_hbm)
    counts_in.wait()
    lane = lax.broadcasted_iota(jnp.int32, (8, 128), 1)
    for i in range(4):
        for j in range(4):
            live[i * 4 + j] = (lane < counts[i, j]).astype(F32)
    send(live, live_hbm)
    coeffs_in.wait()
    for copy in rad_in:
        copy.wait()
    leaves = []
    for i in range(4):
        for j in range(4):
            on = live[i * 4 + j]
            masked = pair(
                coeffs[0, i, j].astype(F32) * on, coeffs[1, i, j].astype(F32) * on
            ).astype(BF16)
            wide = jnp.concatenate([rad[0, i, j], rad[1, i, j]], axis=1)
            prod = jnp.dot(masked, wide, preferred_element_type=F32)
            first, second = prod[:, 0:128], prod[:, 128:256]
            leaf = pair(first[0:8] - second[8:16], first[8:16] + second[0:8]).astype(BF16)
            leaves.append(leaf)
            own[j * 4 + i] = leaf
            own[16 + j * 4 + i] = masked
            if i < 2:
                down[j * 2 + i] = leaf
            else:
                up[j * 2 + i - 2] = leaf
            if i == 0:
                down[8 + j] = masked
            if i == 3:
                up[8 + j] = masked
    for source, target, count in ((up, up_hbm, 12), (down, down_hbm, 12), (own, own_hbm, 32)):
        send(source.at[pl.ds(0, count)], target.at[pl.ds(0, count)])
    interp_in.wait()
    spread = dot_nt(jnp.concatenate(leaves, axis=0), interp[...])
    for big_i in range(2):
        for big_j in range(2):
            real = imag = None
            for a in range(2):
                for b in range(2):
                    at = ((2 * big_i + a) * 4 + 2 * big_j + b) * 16
                    s_re, s_im = spread[at : at + 8], spread[at + 8 : at + 16]
                    c = cosine[2 * a + b : 2 * a + b + 1]
                    s = sine[2 * a + b : 2 * a + b + 1]
                    t_re = c * s_re - s * s_im
                    t_im = c * s_im + s * s_re
                    real = t_re if real is None else real + t_re
                    imag = t_im if imag is None else imag + t_im
            upper = pair(real, imag).astype(BF16)
            for t in range(4):
                own[32 + (big_i * 2 + big_j) * 4 + t] = upper[:, t * 128 : (t + 1) * 128]
    uppers = own.at[pl.ds(32, 16)]
    for target, at in ((up_hbm, 12), (down_hbm, 12), (own_hbm, 32)):
        send(uppers, target.at[pl.ds(at, 16)])
    for copy in sent:
        copy.wait()


def pass_kernel(pieces, same):
    del pieces, same


def pack_kernel(own, before, after, right, left):
    for target, col in ((right, 2), (left, 0)):
        edge_col = 3 if col else 0
        moves = [
            (before, col * 2, 0, 4),
            (own, col * 4, 4, 8),
            (after, col * 2, 12, 4),
            (before, 8 + edge_col, 16, 1),
            (own, 16 + edge_col * 4, 17, 4),
            (after, 8 + edge_col, 21, 1),
            (before, 12, 22, 16),
            (own, 32, 38, 16),
            (after, 12, 54, 16),
        ]
        for source, start, at, size in moves:
            target[at : at + size] = source[start : start + size]


def near_sum(masks, real_blocks, imag_blocks):
    row = jnp.concatenate(masks, axis=1)
    first = dot_nt(row, jnp.concatenate(real_blocks, axis=1))
    second = dot_nt(row, jnp.concatenate(imag_blocks, axis=1))
    return pair(first[0:8] - second[8:16], first[8:16] + second[0:8])


def border_flags():
    box, col = lax.axis_index("box"), lax.axis_index("dir")
    return (
        (box > 0).astype(F32),
        (box < lax.axis_size("box") - 1).astype(F32),
        (col > 0).astype(F32),
        (col < lax.axis_size("dir") - 1).astype(F32),
    )


def masked_unit(unit, flag):
    return (unit.astype(F32) * flag).astype(BF16)


def inside(j):
    return [dy for dy in (-1, 0, 1) if 0 <= j + dy < 4]


def near_kernel(
    own, before, after, trans_leaf, blocks, out, rest, far, held, leaf_halo, sems, rest_sems
):
    copies = []
    for i in range(4):
        group = [pltpu.make_async_copy(blocks.at[:, i, 1:3], held.at[:, i, 1:3], sems.at[i, 0])]
        for j, low in ((0, 1), (3, 0)):
            for dx in range(3):
                span = pl.ds(3 * dx + low, 2)
                group.append(
                    pltpu.make_async_copy(
                        blocks.at[:, i, j, span], held.at[:, i, j, span], sems.at[i, len(group)]
                    )
                )
        copies.append(group)
    for group in copies:
        for copy in group:
            copy.start()
    rest_copies = []
    for side, j in enumerate((0, 3)):
        for dx in range(3):
            slot = side * 3 + dx
            rest_copies.append(
                pltpu.make_async_copy(
                    blocks.at[:, :, j, 3 * dx + 2 * side], rest.at[slot], rest_sems.at[slot]
                )
            )
    for copy in rest_copies:
        copy.start()
    has_before, has_after, _, _ = border_flags()
    rows = {}
    for j in range(4):
        rows[-1, j] = (before[8 + j].astype(F32) * has_before).astype(BF16)
        rows[4, j] = (after[8 + j].astype(F32) * has_after).astype(BF16)
        for i in range(4):
            rows[i, j] = own[16 + j * 4 + i]
    for j in range(4):
        for r in range(2):
            leaf_halo[r * 4 + j] = before[j * 2 + r].astype(F32) * has_before
            leaf_halo[(r + 6) * 4 + j] = after[j * 2 + r].astype(F32) * has_after
        for i in range(4):
            leaf_halo[(i + 2) * 4 + j] = own[j * 4 + i].astype(F32)

    def far_step(big_i, carry):
        for big_j in range(2):
            first = 2 - 2 * big_j
            total = translate(
                lambda r, c: leaf_halo[(big_i * 2 + r) * 4 + c - first],
                lambda dx, dy: leaf_coef(trans_leaf, dx, dy),
                {},
                range(first, first + 4),
            )
            for a, b in CHILDREN:
                far[(big_i * 2 + big_j) * 4 + a * 2 + b] = pair(*total[a, b])
        return carry

    lax.fori_loop(0, 2, far_step, 0)
    for i in range(4):
        for copy in copies[i]:
            copy.wait()
        for j in range(4):
            pairs = [(dx, dy) for dx in (-1, 0, 1) for dy in inside(j)]
            out[i * 4 + j] = near_sum(
                [rows[i + dx, j + dy] for dx, dy in pairs],
                [held[0, i, j, 3 * (dx + 1) + dy + 1] for dx, dy in pairs],
                [held[1, i, j, 3 * (dx + 1) + dy + 1] for dx, dy in pairs],
            )
    for copy in rest_copies:
        copy.wait()


def translate(source, coef, start, cols):
    sums = {}
    for r in range(6):
        units = {}
        for c in cols:
            unit = source(r, c)
            s_re, s_im = unit[0:8], unit[8:16]
            units[c] = (s_re + s_im, s_im, s_re)
        for a in range(2):
            dx = r - 2 - a
            for dy in range(-3, 4):
                targets = [b for b in range(2) if dy + 2 + b in units]
                if max(abs(dx), abs(dy)) < 2 or not targets:
                    continue
                factors = [jnp.broadcast_to(k, (8, 128)) for k in coef(dx, dy)]
                for b in targets:
                    terms = [k * v for k, v in zip(factors, units[dy + 2 + b])]
                    if (a, b) in sums:
                        terms = [old + new for old, new in zip(sums[a, b], terms)]
                    sums[a, b] = terms
    total = {}
    for key, (p, q, w) in sums.items():
        t_re, t_im = p - q, p + w
        if key in start:
            t_re, t_im = start[key][0] + t_re, start[key][1] + t_im
        total[key] = (t_re, t_im)
    return total


def leaf_coef(trans_leaf, dx, dy):
    k_re = trans_leaf[dx + 3, dy + 3, pl.ds(0, 1), :]
    k_im = trans_leaf[dx + 3, dy + 3, pl.ds(1, 1), :]
    return k_re, k_re + k_im, k_im - k_re


CHILDREN = [(a, b) for a in range(2) for b in range(2)]


def middle_kernel(
    own,
    before,
    after,
    left,
    right,
    trans_leaf,
    near,
    rest,
    far_own,
    far,
    upper_halo,
    field,
    leaf_halo,
):
    f_before, f_after, f_left, f_right = border_flags()
    for side, (part, flag) in enumerate(((left, f_left), (right, f_right))):
        for c in range(2):
            for r in range(2):
                leaf_halo[side, r * 2 + c] = part[c * 2 + r].astype(F32) * (flag * f_before)
                leaf_halo[side, (r + 6) * 2 + c] = part[12 + c * 2 + r].astype(F32) * (
                    flag * f_after
                )
            for i in range(4):
                leaf_halo[side, (i + 2) * 2 + c] = part[4 + c * 4 + i].astype(F32) * flag
    for p in range(2):
        for q in range(2):
            for t in range(4):
                unit = (p * 2 + q) * 4 + t
                upper_halo[t, p * 6 + q + 2] = before[12 + unit].astype(F32) * f_before
                upper_halo[t, (p + 2) * 6 + q + 2] = own[32 + unit].astype(F32)
                upper_halo[t, (p + 4) * 6 + q + 2] = after[12 + unit].astype(F32) * f_after
                for part, flag, start in ((left, f_left, 0), (right, f_right, 4)):
                    upper_halo[t, p * 6 + q + start] = part[22 + unit].astype(F32) * (
                        flag * f_before
                    )
                    upper_halo[t, (p + 2) * 6 + q + start] = part[38 + unit].astype(F32) * flag
                    upper_halo[t, (p + 4) * 6 + q + start] = part[54 + unit].astype(F32) * (
                        flag * f_after
                    )

    def far_step(big_i, carry):
        for big_j in range(2):
            first = 4 * big_j
            at = (big_i * 2 + big_j) * 4
            start = {}
            for a, b in CHILDREN:
                unit = far_own[at + a * 2 + b]
                start[a, b] = (unit[0:8], unit[8:16])
            total = translate(
                lambda r, c: leaf_halo[big_j, (big_i * 2 + r) * 2 + c - first],
                lambda dx, dy: leaf_coef(trans_leaf, dx, dy),
                start,
                range(first, first + 2),
            )
            for a, b in CHILDREN:
                far[at + a * 2 + b] = pair(*total[a, b])
        return carry

    lax.fori_loop(0, 2, far_step, 0)

    sides = {}
    for j, part, flag in ((0, left, f_left), (3, right, f_right)):
        sides[j, -1] = masked_unit(part[16], flag * f_before)
        sides[j, 4] = masked_unit(part[21], flag * f_after)
        for i in range(4):
            sides[j, i] = masked_unit(part[17 + i], flag)
    for i in range(4):
        for j in range(4):
            value = near[i * 4 + j]
            if j in (0, 3):
                slots = [(3 if j else 0) + dx for dx in range(3)]
                value = value + near_sum(
                    [sides[j, i + dx] for dx in (-1, 0, 1)],
                    [rest[slot, 0, i] for slot in slots],
                    [rest[slot, 1, i] for slot in slots],
                )
            field[i * 4 + j] = value


def final_kernel(
    live,
    upper_halo,
    pieces,
    far,
    anterp,
    phase,
    near,
    rad,
    out_hbm,
    out,
    table,
    out_sems,
):
    for t in range(4):
        turned = pieces[pl.ds(t * 32, 32)].astype(F32).reshape(128, 128).T
        k_re, k_im = turned[0:56], turned[56:112]
        table[t, 0:56] = k_re
        table[t, 56:112] = k_re + k_im
        table[t, 112:168] = k_im - k_re

    back = None
    for t in range(4):
        total = translate(
            lambda r, c: upper_halo[t, r * 6 + c],
            lambda dx, dy: [
                table[t, pl.ds(part * 56 + (dx + 3) * 8 + dy + 3, 1), :] for part in range(3)
            ],
            {},
            range(6),
        )
        rows = []
        for key in CHILDREN:
            t_re, t_im = (part.astype(BF16).astype(F32) for part in total[key])
            for child in range(4):
                c = phase[child : child + 1, t * 128 : (t + 1) * 128]
                s = phase[4 + child : 5 + child, t * 128 : (t + 1) * 128]
                rows.append(pair(c * t_re + s * t_im, c * t_im - s * t_re).astype(BF16))
        part = dot_nt(jnp.concatenate(rows, axis=0), anterp[:, t * 128 : (t + 1) * 128])
        back = part if back is None else back + part
    sent = []
    for i in range(4):
        for j in range(4):
            at = ((i // 2) * 2 + j // 2) * 4 + (i % 2) * 2 + j % 2
            total = (far[at] + back[at * 16 : at * 16 + 16]).astype(BF16)
            both = dot_nt(total, rad[:, i, j].reshape(256, 128))
            first, second = both[:, 0:128], both[:, 128:256]
            field = near[i * 4 + j] + pair(
                first[0:8] + second[8:16], first[8:16] - second[0:8]
            )
            on = live[i * 4 + j]
            out[0, i, j] = field[0:8] * on
            out[1, i, j] = field[8:16] * on
        sent.append(pltpu.make_async_copy(out.at[:, i], out_hbm.at[:, i], out_sems.at[i]))
        sent[-1].start()
    for copy in sent:
        copy.wait()


def unit_shape(count):
    return jax.ShapeDtypeStruct((count, 16, 128), BF16)


def shards(
    coeffs, counts, radiation, near_blocks, trans_leaf, interp, anterp, shift_angle, trans_top
):
    n_box = lax.axis_size("box")
    n_dir = lax.axis_size("dir")
    devices = n_box * n_dir
    outputs = (
        unit_shape(OWN),
        unit_shape(EDGE),
        unit_shape(EDGE),
        jax.ShapeDtypeStruct((8, 512), F32),
        jax.ShapeDtypeStruct((16, 8, 128), F32),
        jax.ShapeDtypeStruct((devices, 4, 128), BF16),
    )
    own, to_after, to_before, phase, live, pieces = pl.pallas_call(
        leaf_kernel,
        out_shape=outputs,
        in_specs=[hbm()] * 6,
        out_specs=(hbm(),) * 6,
        scratch_shapes=[
            pltpu.SMEM((4, 4), jnp.int32),
            pltpu.VMEM((2, 4, 4, 8, 128), BF16),
            pltpu.VMEM((2, 4, 4, 128, 128), BF16),
            pltpu.VMEM((512, 128), BF16),
            pltpu.VMEM((4, 512), F32),
            pltpu.VMEM((2, 7, 4, 7), F32),
        ]
        + [pltpu.VMEM(out.shape, out.dtype) for out in outputs]
        + [
            pltpu.SemaphoreType.DMA((5,)),
            pltpu.SemaphoreType.DMA((4,)),
            pltpu.SemaphoreType.DMA((9,)),
        ],
        compiler_params=params(62),
        cost_estimate=cost(2),
        name="leaf",
    )(counts, coeffs, radiation, interp, shift_angle, trans_top.transpose(0, 1, 3, 2))
    forward = [(i, (i + 1) % n_box) for i in range(n_box)]
    backward = [((i + 1) % n_box, i) for i in range(n_box)]
    before = lax.ppermute(to_after, "box", forward)
    after = lax.ppermute(to_before, "box", backward)
    pieces = pl.pallas_call(
        pass_kernel,
        out_shape=jax.ShapeDtypeStruct((devices, 4, 128), BF16),
        in_specs=[hbm()],
        out_specs=hbm(),
        input_output_aliases={0: 0},
        compiler_params=params(62),
        cost_estimate=cost(20),
        name="pass",
    )(pieces)
    gathered = lax.all_to_all(pieces, ("box", "dir"), split_axis=0, concat_axis=0, tiled=True)
    to_right, to_left = pl.pallas_call(
        pack_kernel,
        out_shape=(unit_shape(SIDE), unit_shape(SIDE)),
        in_specs=[vmem()] * 3,
        out_specs=(vmem(),) * 2,
        compiler_params=params(4),
        cost_estimate=cost(20),
        name="pack",
    )(own, before, after)
    left = lax.ppermute(to_right, "dir", [(i, (i + 1) % n_dir) for i in range(n_dir)])
    right = lax.ppermute(to_left, "dir", [((i + 1) % n_dir, i) for i in range(n_dir)])
    by_offset = trans_leaf.transpose(1, 2, 0, 3)
    near, rest, far = pl.pallas_call(
        near_kernel,
        out_shape=(
            jax.ShapeDtypeStruct((16, 16, 128), F32),
            jax.ShapeDtypeStruct((6, 2, 4, 128, 128), BF16),
            jax.ShapeDtypeStruct((16, 16, 128), F32),
        ),
        in_specs=[vmem()] * 4 + [hbm()],
        out_specs=(vmem(),) * 3,
        scratch_shapes=[
            pltpu.VMEM((2, 4, 4, 9, 128, 128), BF16),
            pltpu.VMEM((32, 16, 128), F32),
            pltpu.SemaphoreType.DMA((4, 7)),
            pltpu.SemaphoreType.DMA((6,)),
        ],
        compiler_params=params(48),
        cost_estimate=cost(4),
        name="near",
    )(own, before, after, by_offset, near_blocks)
    far, upper_halo, near = pl.pallas_call(
        middle_kernel,
        out_shape=(
            jax.ShapeDtypeStruct((16, 16, 128), F32),
            jax.ShapeDtypeStruct((4, 36, 16, 128), F32),
            jax.ShapeDtypeStruct((16, 16, 128), F32),
        ),
        in_specs=[vmem()] * 9,
        out_specs=(vmem(),) * 3,
        scratch_shapes=[pltpu.VMEM((2, 16, 16, 128), F32)],
        compiler_params=params(48),
        cost_estimate=pl.CostEstimate(flops=10**7, bytes_accessed=1 << 14, transcendentals=0),
        name="middle",
    )(own, before, after, left, right, by_offset, near, rest, far)
    return pl.pallas_call(
        final_kernel,
        out_shape=jax.ShapeDtypeStruct((2, 4, 4, 8, 128), F32),
        in_specs=[vmem()] * 8,
        out_specs=hbm(),
        scratch_shapes=[
            pltpu.VMEM((2, 4, 4, 8, 128), F32),
            pltpu.VMEM((4, 168, 128), F32),
            pltpu.SemaphoreType.DMA((4,)),
        ],
        compiler_params=params(48),
        cost_estimate=cost(4),
        name="final",
    )(live, upper_halo, gathered, far, anterp, phase, near, radiation)


def solution(mesh):
    return jax.shard_map(
        shards,
        mesh=mesh,
        in_specs=(
            P(None, "box", "dir", None, None),
            P("box", "dir"),
            P(None, "box", "dir", None, None),
            P(None, "box", "dir", None, None, None),
            P(),
            P(),
            P(),
            P(),
            P(None, None, None, ("box", "dir")),
        ),
        out_specs=P(None, "box", "dir", None, None),
        check_vma=False,
    )
```
